1024 devices in a mesh: user: 8 (over y), item: 128 (over x, z, core).
Axes of the slice: x: 4, y: 8, z: 16, core: 2. Of those that a mesh axis runs over, the one named last changes fastest.
Arguments:
- features: bfloat16 [262144, 2048], P(('user', 'item')), may hold values from -6 to 6
- w_out: bfloat16 [2048, 256], replicated, may hold values from -0.125 to 0.125
- interests: bfloat16 [65536, 8, 256], P(('user', 'item')), may hold values from -136 to 136
- neg_tiles: int32 [65536, 4], P(('user', 'item')), may hold values from 0 to 15
- positives: int32 [65536], P(('user', 'item')), may hold values from 0 to 2047
- tile_valid: int32 [2048], P(('user', 'item')), may hold values from 1 to 128
Outputs:
- grad_w: float32 [2048, 256], P('item')
- grad_interests: float32 [65536, 8, 256], P(('user', 'item'))
- user_loss: float32 [65536], P(('user', 'item'))
The draws below stay inside these ranges and needn't reach their ends.
Inputs may be any that keep to these rules, and one draw needn't show every extreme that they name: `neg_tiles`: tile numbers within the user's group. `positives`: item numbers within the user's group. `tile_valid`: live slots are the first ones of a tile.
All inputs are finite; a program needn't handle non-finite values.
Results may differ from the reference program's by a relative error of at most 0.012.
The reference program's roundings to bfloat16 on the way (of `embedded`, `catalogue`, `score_grad` and `item_grad`) count: a program that leaves them out, or rounds other values in their place, can miss the bound.
Values may be sent and summed in bfloat16 or wider, within the bound.
A program may use at most 32 MiB of HBM per device.

```python
import math
import jax
import jax.numpy as jnp
import numpy as np
from jax import lax

H = 2048
E = 256
K = 8
TILE = 128
NT = 4
TILES_DEV = 2
U_DEV = 64
ITEM_DEV = 256
ITEMS = 262144
TILES = 2048
USERS = 65536
GROUP_TILES = 16
GROUP_ITEMS = 2048
N_USER = 8
N_ITEM = 128


def draw_interests(key, part):
    key = jax.random.fold_in(key, 11)
    first_key = jax.random.fold_in(key, 0)
    base = jax.random.normal(first_key, (USERS, K, E), jnp.float32)
    return jnp.clip(base, -6.0, 6.0).astype(jnp.bfloat16)


def with_ends(result, stream_key, least, largest):
    dims = result.shape
    spot = [jax.random.randint(jax.random.fold_in(stream_key, axis), (), 0, dims[axis]) for axis in range(len(dims))]
    result = result.at[tuple(spot)].set(least)
    longest = dims.index(max(dims))
    spot[longest] = (spot[longest] + 1) % dims[longest]
    return result.at[tuple(spot)].set(largest)


def block_levels(own_key, dims, cuts, smallest, top_value):
    factor_of = 1.0
    for dim, parts in cuts:
        draws = jax.random.uniform(jax.random.fold_in(jax.random.fold_in(own_key, 6), dim), (parts,), jnp.float32, smallest / len(cuts), top_value / len(cuts))
        factor_of = factor_of * jnp.repeat(jnp.exp(draws), dims[dim] // parts).reshape((-1,) + (1,) * (len(dims) - 1 - dim))
    return factor_of


def rank_bounds(amount, lean):
    weights = [(1 << 20) // math.isqrt(standing ** lean) + 1 for standing in range(1, amount + 1)]
    scale = 1 + sum(weights) // (1 << 30)
    return np.cumsum(np.array([max(1, weight // scale) for weight in weights]))


def ranked_ids(own_key, shape, number_of, skew):
    table = rank_bounds(number_of, skew)
    ticket = jax.random.randint(jax.random.fold_in(own_key, 1), shape, 0, int(table[number_of - 1]))
    rank = jnp.searchsorted(jnp.asarray(table, jnp.int32), ticket, side="right")
    return jax.random.permutation(jax.random.fold_in(own_key, 2), number_of)[rank].astype(jnp.int32)


def gaussian(own_key, extent, deviation, bound, pieces=(), kind=jnp.bfloat16):
    result = jax.random.normal(own_key, extent, jnp.float32) * deviation
    if len(pieces) > 0:
        result = block_levels(own_key, extent, pieces, -0.22, 0.18) * result
    return jnp.clip(result, min=-bound, max=bound).astype(kind)


def setup_inputs(seed: int = 0) -> dict:
    streams_of = jax.random.split(jax.random.key(seed), 7)
    return {
        "features": gaussian(streams_of[0], (ITEMS, H), 1.0, 6.0, ((0, 1024),)),
        "w_out": gaussian(streams_of[1], (H, E), H ** -0.5, 0.125),
        "interests": draw_interests(jax.random.fold_in(streams_of[6], 71), 0),
        "neg_tiles": with_ends(ranked_ids(streams_of[3], (USERS, NT), GROUP_TILES, 2), jax.random.fold_in(streams_of[3], 3), 0, GROUP_TILES - 1).astype(jnp.int32),
        "positives": with_ends(jax.random.randint(streams_of[4], (USERS,), 0, GROUP_ITEMS), jax.random.fold_in(streams_of[4], 1), 0, GROUP_ITEMS - 1).astype(jnp.int32),
        "tile_valid": with_ends(jax.random.randint(streams_of[5], (TILES,), 1, TILE + 1), jax.random.fold_in(streams_of[5], 1), 1, TILE).astype(jnp.int32),
    }


def block_terms(catalogue, counts, queries, negatives, positive_ids):
    tile_count = counts.shape[0]
    item_count = catalogue.shape[0]
    user_count = queries.shape[0]
    scores = jnp.einsum('uke,ge->ukg', queries.astype(jnp.float32), catalogue.astype(jnp.float32)) * (E ** -0.5)
    tile_hits = jnp.sum((negatives[:, :, None] == jnp.arange(tile_count, dtype=jnp.int32)[None, None, :]).astype(jnp.float32), axis=1)
    live_mask = (jnp.arange(TILE, dtype=jnp.int32)[None, :] < counts[:, None]).astype(jnp.float32)
    weight = (tile_hits[:, :, None] * live_mask[None]).reshape(user_count, 1, item_count)
    onehot = (jnp.arange(item_count, dtype=jnp.int32)[None, :] == positive_ids[:, None]).astype(jnp.float32).reshape(user_count, 1, item_count)
    pos_score = jnp.sum(onehot * scores, axis=-1)
    chosen = weight > 0
    highest = jnp.maximum(pos_score, jnp.max(jnp.where(chosen, scores, -jnp.inf), axis=-1))
    exp_terms = weight * jnp.exp(jnp.where(chosen, scores - highest[..., None], 0.0))
    pos_term = jnp.exp(pos_score - highest)
    denominator = pos_term + jnp.sum(exp_terms, axis=-1)
    user_loss = jnp.sum(highest + jnp.log(denominator) - pos_score, axis=-1)
    score_grad = (exp_terms / denominator[..., None] + onehot * (pos_term / denominator - 1.0)[..., None]).astype(jnp.bfloat16)
    query_grads = jnp.einsum('ukg,ge->uke', score_grad.astype(jnp.float32), catalogue.astype(jnp.float32))
    item_part = jnp.einsum('ukg,uke->ge', score_grad.astype(jnp.float32), queries.astype(jnp.float32))
    return user_loss, query_grads, item_part


def reference(features, w_out, interests, neg_tiles, positives, tile_valid):
    embedded = jnp.dot(features, w_out, preferred_element_type=jnp.float32).astype(jnp.bfloat16)
    groups = embedded.reshape(N_USER, N_ITEM, ITEM_DEV, E).transpose(1, 0, 2, 3).reshape(N_ITEM, GROUP_ITEMS, E)
    counts = tile_valid.reshape(N_USER, N_ITEM, TILES_DEV).transpose(1, 0, 2).reshape(N_ITEM, GROUP_TILES)
    queries = interests.reshape(N_USER, N_ITEM, U_DEV, K, E).transpose(1, 0, 2, 3, 4)
    negatives = neg_tiles.reshape(N_USER, N_ITEM, U_DEV, NT).transpose(1, 0, 2, 3)
    positive_ids = positives.reshape(N_USER, N_ITEM, U_DEV).transpose(1, 0, 2)

    def per_group(packed):
        catalogue, group_counts, group_queries, group_negatives, group_positives = packed

        def advance(running, blocks):
            user_loss, query_grads, item_part = block_terms(catalogue, group_counts, blocks[0], blocks[1], blocks[2])
            rounded = lax.optimization_barrier(item_part.astype(jnp.bfloat16))
            return running + rounded.astype(jnp.float32), (user_loss, query_grads)

        start_sum = jnp.zeros((GROUP_ITEMS, E), jnp.float32)
        summed, outputs = lax.scan(advance, start_sum, (group_queries, group_negatives, group_positives))
        return summed.astype(jnp.bfloat16), outputs[0], outputs[1]

    item_grad, losses, query_grads = lax.map(per_group, (groups, counts, queries, negatives, positive_ids))
    item_grad = item_grad.reshape(N_ITEM, N_USER, ITEM_DEV, E).transpose(1, 0, 2, 3).reshape(ITEMS, E)
    grad_w = jnp.dot(features.T, item_grad, preferred_element_type=jnp.float32)
    user_loss = losses.transpose(1, 0, 2).reshape(USERS)
    grad_interests = query_grads.transpose(1, 0, 2, 3, 4).reshape(USERS, K, E)
    return grad_w, grad_interests, user_loss
```

```python
import functools
from types import SimpleNamespace

import jax
import jax.numpy as jnp
from jax import lax
from jax.experimental import pallas as pl
from jax.experimental.pallas import tpu as pltpu
from jax.sharding import PartitionSpec as P

MESH = pl.DeviceIdType.MESH
NX, NZ, NC = 4, 16, 2
TILE = 128
DEPTHS = 4
PIECES = 4
ROWS = 32
LOW = -1e30
F32, BF16 = jnp.float32, jnp.bfloat16

NAMES = (
    "features", "w_out", "interests", "negatives", "positives", "valid",
    "grad_w", "grad_interests", "user_loss",
    "feat", "feat_t", "w", "q", "qs", "cat", "cnt", "neg_rows", "expo", "prob", "m_rows", "l_rows", "p_rows",
    "query_grad", "item_part", "item_grad",
    "ring_up", "ring_down", "feat_s", "item_sib", "w_own", "x_two", "x_up", "x_down", "x_own", "xr_two_up",
    "xr_two_down", "xr_up", "xr_down",
    "y_send", "y_own", "y_recv", "z_send", "z_own", "z_recv", "g_buf",
    "local_sem", "cnt_send", "cnt_recv", "gather_send", "gather_recv", "ring_send", "ring_recv", "core_send",
    "core_recv",
    "x_send", "x_recv", "y_ssem", "y_rsem", "z_ssem", "z_rsem", "g_ssem", "g_rsem",
)


def dot(a, b, dims):
    return lax.dot_general(a, b, ((dims[:1], dims[1:]), ((), ())), preferred_element_type=F32)


def kernel(ny, *refs):
    r = SimpleNamespace(**dict(zip(NAMES, refs, strict=True)))
    half = ny // 2
    users, kk = r.positives.shape[1], r.q.shape[0] // r.positives.shape[1]
    lanes = users * kk
    items = r.feat.shape[0]
    y = lax.axis_index("user")
    item = lax.axis_index("item")
    core = lax.rem(item, NC)
    z = lax.rem(item // NC, NZ)
    x = item // (NC * NZ)

    def at(y2, x2, z2, c2):
        return (y2, (x2 * NZ + z2) * NC + c2)

    def y_peer(d):
        return at(lax.rem(y + d + ny, ny), x, z, core)

    def x_peer(d):
        return at(y, lax.rem(x + d + NX, NX), z, core)

    def z_peer(d):
        return at(y, x, lax.rem(z + d, NZ), core)

    sibling = at(y, x, z, 1 - core)
    pending = []

    def send(src, dst, send_sem, recv_sem, device):
        copy = pltpu.make_async_remote_copy(
            src_ref=src, dst_ref=dst, send_sem=send_sem, recv_sem=recv_sem, device_id=device, device_id_type=MESH
        )
        copy.start()
        pending.append(copy)
        return copy

    depth = r.feat.shape[1] // DEPTHS
    parts_w, parts_f = [], []
    for i in range(DEPTHS):
        cut = pl.ds(i * depth, depth)
        parts_w.append(pltpu.make_async_copy(r.w_out.at[cut], r.w.at[cut], r.local_sem.at[2 + 2 * i]))
        parts_f.append(pltpu.make_async_copy(r.features.at[:, cut], r.feat.at[:, cut], r.local_sem.at[3 + 2 * i]))
        parts_w[i].start()
        parts_f[i].start()
    copy_q = pltpu.make_async_copy(r.interests, r.q, r.local_sem.at[0])
    copy_q.start()
    barrier = pltpu.get_barrier_semaphore()

    def greet(device):
        pl.semaphore_signal(barrier, inc=1, device_id=device, device_id_type=MESH)

    for d in range(1, ny):
        greet(y_peer(d))
    greet(sibling)
    greet(x_peer(1))
    greet(x_peer(-1))

    def greet_z(d, carry):
        greet(z_peer(d))
        return carry

    lax.fori_loop(1, NZ, greet_z, 0)

    own_counts = jnp.where(lax.broadcasted_iota(jnp.int32, (8, TILE), 0) == 0, r.valid[0], r.valid[1])
    r.cnt[y] = own_counts
    embedded = jnp.zeros((items, r.w.shape[1]), F32)
    for i in range(DEPTHS):
        parts_w[i].wait()
        parts_f[i].wait()
        cut = slice(i * depth, (i + 1) * depth)
        embedded = embedded + dot(r.feat[:, cut], r.w[cut, :], (1, 0))
    r.cat[0:2] = embedded.astype(BF16).reshape(2, TILE, r.w.shape[1])
    pl.semaphore_wait(barrier, (ny - 1) + 1 + 2 + (NZ - 1))

    gather = {}

    piece = 2 * TILE // PIECES
    per_tile = PIECES // 2

    def pass_on(up, step, part):
        here, there = (step - 1, step) if up else ((ny - step + 1) % ny, ny - step)
        way, slot = (0 if up else 1), PIECES * (step - 1) + part
        rows = pl.ds(part % per_tile * piece, piece)
        tile = part // per_tile
        gather[up, step, part] = send(
            r.cat.at[2 * here + tile, rows],
            r.cat.at[2 * there + tile, rows],
            r.gather_send.at[way, slot],
            r.gather_recv.at[way, slot],
            y_peer(1 if up else -1),
        )

    for part in range(PIECES):
        pass_on(True, 1, part)
        pass_on(False, 1, PIECES - 1 - part)
    counts = [
        send(r.cnt.at[y], r.cnt.at[y], r.cnt_send.at[d], r.cnt_recv.at[d], y_peer(d)) for d in range(1, ny)
    ]

    copy_q.wait()
    r.qs[...] = (r.q[...].astype(F32) * r.q.shape[1] ** -0.5).astype(BF16)
    owner_of_lane = lax.broadcasted_iota(jnp.int32, (users, lanes), 1) // kk
    of_user = owner_of_lane == lax.broadcasted_iota(jnp.int32, (users, lanes), 0)
    diagonal = lax.broadcasted_iota(jnp.int32, (users, users), 0) == lax.broadcasted_iota(
        jnp.int32, (users, users), 1
    )

    def to_lanes(column):
        return jnp.sum(jnp.where(of_user, column, 0.0), axis=0, keepdims=True)

    def to_row(values):
        spread = jnp.broadcast_to(values.astype(F32), (users, users))
        column = jnp.sum(jnp.where(diagonal, spread, 0.0), axis=1, keepdims=True)
        return to_lanes(column).astype(jnp.int32)

    n_neg = r.negatives.shape[0]
    for j in range(n_neg):
        r.neg_rows[j : j + 1, :] = to_row(r.negatives[j : j + 1, :])
    pos_row = to_row(r.positives[...])

    def origin(block):
        return lax.rem(y - block + ny, ny)

    def positive_slot(block, tile):
        first = (origin(block) * 2 + tile) * TILE
        return pos_row - first

    def fold(values, op):
        parts = values.reshape(ROWS // 8, 8, lanes)
        return op(parts, axis=0)

    def row_ids(i):
        return lax.broadcasted_iota(jnp.int32, (ROWS, lanes), 0) + i * ROWS

    counted = {0}

    def score_tile(block, tile):
        if block not in counted:
            counts[block - 1].wait_recv()
            counted.add(block)
        u = origin(block)
        index = 2 * block + tile
        first = tile * TILE
        r.expo[block, first : first + TILE, :] = dot(r.cat[index], r.qs[...], (1, 1))
        number = u * 2 + tile
        hit = jnp.zeros((1, lanes), F32)
        for j in range(n_neg):
            hit = hit + jnp.where(r.neg_rows[j : j + 1, :] == number, 1.0, 0.0)
        live = r.cnt[u][tile : tile + 1, :]
        live = jnp.concatenate([live] * (lanes // TILE), axis=1)
        live = jnp.where(hit > 0, live, 0)
        slot = positive_slot(block, tile)

        def mask(i, carry):
            peak, picked = carry
            rows = pl.ds(first + i * ROWS, ROWS)
            s = r.expo[block, rows, :]
            ids = row_ids(i)
            kept = jnp.where(ids < live, s, LOW)
            r.expo[block, rows, :] = kept
            picked = picked + fold(jnp.where(ids == slot, s, 0.0), jnp.sum)
            return jnp.maximum(peak, fold(kept, jnp.max)), picked

        peak, picked = lax.fori_loop(
            0, TILE // ROWS, mask, (jnp.full((8, lanes), LOW, F32), jnp.zeros((8, lanes), F32))
        )
        m = jnp.max(peak, axis=0, keepdims=True)

        def exponent(i, total):
            rows = pl.ds(first + i * ROWS, ROWS)
            e = hit * jnp.exp(r.expo[block, rows, :] - m)
            r.expo[block, rows, :] = e
            return total + fold(e, jnp.sum)

        total = lax.fori_loop(0, TILE // ROWS, exponent, jnp.zeros((8, lanes), F32))
        r.m_rows[index : index + 1, :] = m
        r.l_rows[index : index + 1, :] = jnp.sum(total, axis=0, keepdims=True)
        r.p_rows[index : index + 1, :] = jnp.sum(picked, axis=0, keepdims=True)

    def transpose_features(x2):
        depth = r.feat.shape[1] // NX
        turned = r.feat[:, x2 * depth : (x2 + 1) * depth].T.reshape(NZ, NC, 16, items)
        for c in range(NC):
            part = turned[:, c].reshape(NZ * 16, items)
            r.feat_t[c, x2 * NZ * 16 : (x2 + 1) * NZ * 16, :] = part

    score_tile(0, 0)
    score_tile(0, 1)
    ready = []
    turns = list(range(NX))
    for step in range(1, half + 1):
        for i in range(PIECES if step < half else per_tile):
            for up, part in ((True, i), (False, PIECES - 1 - i)):
                gather[up, step, part].wait_recv()
                if step + 1 < half or (step + 1 == half and i < per_tile):
                    pass_on(up, step + 1, part)
            if ready:
                score_tile(*ready.pop(0))
            if turns:
                transpose_features(turns.pop(0))
            if i % per_tile == per_tile - 1:
                ready += [(step, i // per_tile), ((ny - step) % ny, 1 - i // per_tile)]
    for x2 in turns:
        transpose_features(x2)
    feat_copy = send(r.feat_t.at[1 - core], r.feat_s, r.core_send.at[2], r.core_recv.at[2], sibling)
    for block, tile in ready:
        score_tile(block, tile)
    m_all = r.m_rows[...]
    pos_score = jnp.sum(r.p_rows[...], axis=0, keepdims=True)
    highest = jnp.maximum(pos_score, jnp.max(m_all, axis=0, keepdims=True))
    factor = jnp.exp(m_all - highest)
    pos_term = jnp.exp(pos_score - highest)
    denominator = pos_term + jnp.sum(factor * r.l_rows[...], axis=0, keepdims=True)
    r.m_rows[...] = factor / denominator
    pos_grad = pos_term / denominator - 1.0

    def grad_block(block):
        for tile in range(2):
            share = r.m_rows[2 * block + tile : 2 * block + tile + 1, :]
            slot = positive_slot(block, tile)

            def normalise(i, carry, tile=tile, slot=slot, share=share):
                first = tile * TILE + i * ROWS
                e = r.expo[block, pl.ds(first, ROWS), :]
                g = e * share + jnp.where(row_ids(i) == slot, pos_grad, 0.0)
                r.prob[pl.ds(block * 2 * TILE + first, ROWS), :] = g.astype(BF16)
                return carry

            lax.fori_loop(0, TILE // ROWS, normalise, 0)
        part = dot(r.prob[block * 2 * TILE : (block + 1) * 2 * TILE, :], r.q[...], (1, 0)).astype(BF16)
        r.item_part[block, 0] = part[:, :TILE]
        r.item_part[block, 1] = part[:, TILE:]

    arms = {}

    def own_block(up, k):
        return (ny - half + k) if up else (half - k)

    part_rows = items // 2

    def landing(up, k, h, v):
        return (r.ring_up if up else r.ring_down).at[2 * k + h, pl.ds(v * part_rows, part_rows)]

    def ring(up, k, h, v):
        way = 0 if up else 1
        slot = 4 * k + 2 * h + v
        arms[up, k, h, v] = send(
            r.item_part.at[own_block(up, k) % ny, h, pl.ds(v * part_rows, part_rows)],
            landing(up, k, h, v),
            r.ring_send.at[way, slot],
            r.ring_recv.at[way, slot],
            y_peer(1 if up else -1),
        )

    def arrived(up, k, h, v):
        arms[up, k, h, v].wait_recv()
        return landing(up, k, h, v)[...].astype(F32)

    def add_and_ring(up, k, h):
        block = own_block(up, k) % ny
        for v in range(2):
            own = r.item_part.at[block, h, pl.ds(v * part_rows, part_rows)]
            own[...] = (own[...].astype(F32) + arrived(up, k - 1, h, v)).astype(BF16)
            ring(up, k, h, v)

    def ring_own(up, k, h):
        for v in range(2):
            ring(up, k, h, v)

    grad_block(half)
    ring_own(True, 0, 0)
    ring_own(False, 0, 1)
    grad_block(own_block(True, 1))
    ring_own(True, 1, 1)
    grad_block(own_block(False, 1))
    ring_own(False, 1, 0)
    grad_block(own_block(True, 2))
    add_and_ring(True, 1, 0)
    add_and_ring(False, 1, 1)
    grad_block(own_block(False, 2))

    def query_part(blocks, first):
        rows = 2 * TILE
        total = None
        for block in blocks:
            c = r.cat[2 * block : 2 * block + 2].reshape(rows, r.q.shape[1])
            part = dot(r.prob[block * rows : (block + 1) * rows, :], c, (0, 0))
            total = part if total is None else total + part
        r.query_grad[...] = total if first else r.query_grad[...] + total

    for k in range(2, half):
        add_and_ring(True, k, 1)
        add_and_ring(False, k, 0)
        if k + 1 < half:
            grad_block(own_block(True, k + 1))
        else:
            query_part(range(half - 2, half + 1), True)
        add_and_ring(True, k, 0)
        add_and_ring(False, k, 1)
        if k + 1 < half:
            grad_block(own_block(False, k + 1))
    grad_block(0)
    copy_g = pltpu.make_async_copy(r.query_grad, r.grad_interests, r.local_sem.at[1])
    others = [b for b in range(ny) if not half - 2 <= b <= half]
    query_part(others[:2], False)

    def finish_queries():
        query_part(others[2:], False)
        copy_g.start()
        loss_row = highest + jnp.log(denominator) - pos_score
        loss_column = jnp.sum(jnp.where(of_user, loss_row, 0.0), axis=1, keepdims=True)
        r.user_loss[...] = jnp.sum(jnp.where(diagonal, loss_column, 0.0), axis=0, keepdims=True)

    block_rows = NZ * 16
    mid = block_rows // 2
    core_copy, x_copy = {}, {}

    def weight_part(h):
        parts = []
        for v in range(2):
            own = r.item_part[0, h, v * part_rows : (v + 1) * part_rows, :].astype(F32)
            parts.append(own + arrived(True, half - 1, h, v) + arrived(False, half - 1, h, v))
        item_grad = jnp.concatenate(parts, axis=0).astype(BF16)
        r.item_grad[h] = item_grad
        core_copy[h] = send(r.item_grad.at[h], r.item_sib.at[h], r.core_send.at[h], r.core_recv.at[h], sibling)

    def x_send(h, kind, src, dst, up):
        x_copy[h, kind] = send(src, dst, r.x_send.at[h, kind], r.x_recv.at[h, kind], x_peer(1 if up else -1))

    def x_first(h):
        r.w_own[h] = dot(r.feat_t[core], r.item_grad[h], (1, 0))
        if h == 0:
            feat_copy.wait_recv()
        core_copy[h].wait_recv()
        r.w_own[h] = r.w_own[h] + dot(r.feat_s[...], r.item_sib[h], (1, 0))

        def block_of(owner):
            rows = pl.ds(pl.multiple_of(lax.rem(owner + NX, NX) * block_rows, block_rows), block_rows)
            return r.w_own[h, rows, :]

        r.x_two[h] = block_of(x + 2).astype(BF16)
        x_send(h, 0, r.x_two.at[h, pl.ds(0, mid)], r.xr_two_up.at[h], True)
        x_send(h, 1, r.x_two.at[h, pl.ds(mid, mid)], r.xr_two_down.at[h], False)
        r.x_up[h] = block_of(x + 1).astype(BF16)
        x_send(h, 2, r.x_up.at[h, pl.ds(mid, mid)], r.xr_up.at[h, pl.ds(mid, mid)], True)
        r.x_down[h] = block_of(x - 1).astype(BF16)
        x_send(h, 3, r.x_down.at[h, pl.ds(0, mid)], r.xr_down.at[h, pl.ds(0, mid)], False)
        r.x_own[h] = block_of(x)

    def x_second(h):
        x_copy[h, 0].wait_recv()
        r.x_up[h, pl.ds(0, mid)] = (r.x_up[h, pl.ds(0, mid)].astype(F32) + r.xr_two_up[h].astype(F32)).astype(BF16)
        x_send(h, 4, r.x_up.at[h, pl.ds(0, mid)], r.xr_up.at[h, pl.ds(0, mid)], True)
        x_copy[h, 1].wait_recv()
        r.x_down[h, pl.ds(mid, mid)] = (
            r.x_down[h, pl.ds(mid, mid)].astype(F32) + r.xr_two_down[h].astype(F32)
        ).astype(BF16)
        x_send(h, 5, r.x_down.at[h, pl.ds(mid, mid)], r.xr_down.at[h, pl.ds(mid, mid)], False)

    per_y = NZ // ny

    def y_stage(h):
        for kind in (2, 3, 4, 5):
            x_copy[h, kind].wait_recv()
        total = (r.x_own[h] + r.xr_up[h].astype(F32) + r.xr_down[h].astype(F32)).reshape(ny, per_y, 16, TILE)
        r.y_own[h] = total
        r.y_send[h] = total.astype(BF16)
        y_copy[h] = [
            send(
                r.y_send.at[h, lax.rem(y + d, ny)], r.y_recv.at[h, d], r.y_ssem.at[h, d], r.y_rsem.at[h, d], y_peer(d)
            )
            for d in range(1, ny)
        ]

    def z_copy(h, i, sender):
        owner = y * per_y + i
        return pltpu.make_async_remote_copy(
            src_ref=r.z_send.at[h, i],
            dst_ref=r.z_recv.at[h, sender],
            send_sem=r.z_ssem.at[h, i],
            recv_sem=r.z_rsem.at[h, sender],
            device_id=at(y, x, owner, core),
            device_id_type=MESH,
        )

    def z_stage(h):
        total = r.y_own[h, y]
        for d, copy in enumerate(y_copy[h], 1):
            copy.wait_recv()
            total = total + r.y_recv[h, d].astype(F32)
        r.z_own[h] = total
        r.z_send[h] = total.astype(BF16)
        for i in range(per_y):

            @pl.when(z != y * per_y + i)
            def _(i=i):
                z_copy(h, i, z).start()

    owns = z // per_y == y

    def g_copy(h, d):
        return pltpu.make_async_remote_copy(
            src_ref=r.g_buf.at[h],
            dst_ref=r.g_buf.at[h],
            send_sem=r.g_ssem.at[h, d],
            recv_sem=r.g_rsem.at[h],
            device_id=y_peer(d),
            device_id_type=MESH,
        )

    def g_stage(h):
        @pl.when(owns)
        def _():
            def add(d, total):
                sender = lax.rem(z + d, NZ)
                z_copy(h, 0, sender).wait_recv()
                return total + r.z_recv[h, sender].astype(F32)

            r.g_buf[h] = lax.fori_loop(1, NZ, add, r.z_own[h, lax.rem(z, per_y)])
            for d in range(1, ny):
                g_copy(h, d).start()

    def finish(h):
        @pl.when(jnp.logical_not(owns))
        def _():
            g_copy(h, 1).wait_recv()

        r.grad_w[:, h * TILE : (h + 1) * TILE] = r.g_buf[h]

    y_copy = {}
    for stage in (weight_part, x_first, x_second, y_stage, z_stage, g_stage, finish):
        for h in range(2):
            stage(h)
        if stage is x_first:
            finish_queries()

    for copy in pending:
        copy.wait_send()

    for h in range(2):
        for i in range(per_y):

            @pl.when(z != y * per_y + i)
            def _(h=h, i=i):
                z_copy(h, i, z).wait_send()

    @pl.when(owns)
    def _():
        for h in range(2):
            for d in range(1, ny):
                g_copy(h, d).wait_send()

    copy_g.wait()


def local(ny, features, w_out, interests, neg_tiles, positives, tile_valid):
    items, depth = features.shape
    width = w_out.shape[1]
    users, kk, _ = interests.shape
    lanes = users * kk
    rows = depth // (NX * NZ * NC)
    half_rows = NX * NZ * rows
    block = NZ * rows
    vmem, dma = pltpu.VMEM, pltpu.SemaphoreType.DMA
    scratch = [
        vmem((items, depth), BF16),
        vmem((NC, half_rows, items), BF16),
        vmem((depth, width), BF16),
        vmem((lanes, width), BF16),
        vmem((lanes, width), BF16),
        vmem((2 * ny, TILE, width), BF16),
        vmem((ny, 8, TILE), jnp.int32),
        vmem((8, lanes), jnp.int32),
        vmem((ny, items, lanes), F32),
        vmem((ny * items, lanes), BF16),
        vmem((2 * ny, lanes), F32),
        vmem((2 * ny, lanes), F32),
        vmem((2 * ny, lanes), F32),
        vmem((lanes, width), F32),
        vmem((ny, 2, items, TILE), BF16),
        vmem((2, items, TILE), BF16),
        vmem((ny, items, TILE), BF16),
        vmem((ny, items, TILE), BF16),
        vmem((half_rows, items), BF16),
        vmem((2, items, TILE), BF16),
        vmem((2, half_rows, TILE), F32),
        vmem((2, block, TILE), BF16),
        vmem((2, block, TILE), BF16),
        vmem((2, block, TILE), BF16),
        vmem((2, block, TILE), F32),
        vmem((2, block // 2, TILE), BF16),
        vmem((2, block // 2, TILE), BF16),
        vmem((2, block, TILE), BF16),
        vmem((2, block, TILE), BF16),
        vmem((2, ny, NZ // ny, rows, TILE), BF16),
        vmem((2, ny, NZ // ny, rows, TILE), F32),
        vmem((2, ny, NZ // ny, rows, TILE), BF16),
        vmem((2, NZ // ny, rows, TILE), BF16),
        vmem((2, NZ // ny, rows, TILE), F32),
        vmem((2, NZ, rows, TILE), BF16),
        vmem((2, rows, TILE), F32),
        dma((2 + 2 * DEPTHS,)),
        dma((ny,)),
        dma((ny,)),
        dma((2, PIECES * ny // 2)),
        dma((2, PIECES * ny // 2)),
        dma((2, 2 * ny)),
        dma((2, 2 * ny)),
        dma((3,)),
        dma((3,)),
        dma((2, 6)),
        dma((2, 6)),
        dma((2, ny)),
        dma((2, ny)),
        dma((2, NZ // ny)),
        dma((2, NZ)),
        dma((2, ny)),
        dma((2,)),
    ]
    hbm = pl.BlockSpec(memory_space=pl.ANY)
    in_vmem = pl.BlockSpec(memory_space=pltpu.VMEM)
    grad_w, query_grads, loss = pl.pallas_call(
        functools.partial(kernel, ny),
        out_shape=(
            jax.ShapeDtypeStruct((rows, width), F32),
            jax.ShapeDtypeStruct((lanes, width), F32),
            jax.ShapeDtypeStruct((1, users), F32),
        ),
        in_specs=[hbm, hbm, hbm, in_vmem, in_vmem, pl.BlockSpec(memory_space=pltpu.SMEM)],
        out_specs=(in_vmem, hbm, in_vmem),
        scratch_shapes=scratch,
        compiler_params=pltpu.CompilerParams(
            collective_id=0, has_side_effects=True, vmem_limit_bytes=53 * 1024 * 1024
        ),
    )(features, w_out, interests.reshape(lanes, width), neg_tiles.T, positives.reshape(1, users), tile_valid)
    return grad_w, query_grads.reshape(users, kk, width), loss.reshape(users)


def solution(mesh):
    in_specs = (
        P(("user", "item"), None),
        P(),
        P(("user", "item"), None, None),
        P(("user", "item"), None),
        P(("user", "item")),
        P(("user", "item")),
    )
    out_specs = (P("item", None), P(("user", "item"), None, None), P(("user", "item")))
    body = functools.partial(local, mesh.shape["user"])
    return jax.shard_map(body, mesh=mesh, in_specs=in_specs, out_specs=out_specs, check_vma=False)
```

```python
import functools
from types import SimpleNamespace

import jax
import jax.numpy as jnp
from jax import lax
from jax.experimental import pallas as pl
from jax.experimental.pallas import tpu as pltpu
from jax.sharding import PartitionSpec as P

MESH = pl.DeviceIdType.MESH
NX, NZ, NC = 4, 16, 2
TILE = 128
DEPTHS = 4
PIECES = 4
ROWS = 32
LOW = -1e30
F32, BF16 = jnp.float32, jnp.bfloat16

NAMES = (
    "features", "w_out", "interests", "negatives", "positives", "valid",
    "grad_w", "grad_interests", "user_loss",
    "feat", "feat_t", "w", "q", "qs", "cat", "cnt", "neg_rows", "expo", "prob", "m_rows", "l_rows", "p_rows",
    "query_grad", "item_part", "item_grad",
    "ring_up", "ring_down", "feat_s", "item_sib", "w_own", "x_two", "x_up", "x_down", "x_own", "xr_two_up",
    "xr_two_down", "xr_up", "xr_down",
    "y_send", "y_own", "y_recv", "z_send", "z_own", "z_recv", "g_buf",
    "local_sem", "cnt_send", "cnt_recv", "gather_send", "gather_recv", "ring_send", "ring_recv", "core_send",
    "core_recv",
    "x_send", "x_recv", "y_ssem", "y_rsem", "z_ssem", "z_rsem", "g_ssem", "g_rsem",
)


def dot(a, b, dims):
    return lax.dot_general(a, b, ((dims[:1], dims[1:]), ((), ())), preferred_element_type=F32)


def kernel(ny, *refs):
    r = SimpleNamespace(**dict(zip(NAMES, refs, strict=True)))
    half = ny // 2
    users, kk = r.positives.shape[1], r.q.shape[0] // r.positives.shape[1]
    lanes = users * kk
    items = r.feat.shape[0]
    y = lax.axis_index("user")
    item = lax.axis_index("item")
    core = lax.rem(item, NC)
    z = lax.rem(item // NC, NZ)
    x = item // (NC * NZ)

    def at(y2, x2, z2, c2):
        return (y2, (x2 * NZ + z2) * NC + c2)

    def y_peer(d):
        return at(lax.rem(y + d + ny, ny), x, z, core)

    def x_peer(d):
        return at(y, lax.rem(x + d + NX, NX), z, core)

    def z_peer(d):
        return at(y, x, lax.rem(z + d, NZ), core)

    sibling = at(y, x, z, 1 - core)
    pending = []

    def send(src, dst, send_sem, recv_sem, device):
        copy = pltpu.make_async_remote_copy(
            src_ref=src, dst_ref=dst, send_sem=send_sem, recv_sem=recv_sem, device_id=device, device_id_type=MESH
        )
        copy.start()
        pending.append(copy)
        return copy

    depth = r.feat.shape[1] // DEPTHS
    parts_w, parts_f = [], []
    for i in range(DEPTHS):
        cut = pl.ds(i * depth, depth)
        parts_w.append(pltpu.make_async_copy(r.w_out.at[cut], r.w.at[cut], r.local_sem.at[2 + 2 * i]))
        parts_f.append(pltpu.make_async_copy(r.features.at[:, cut], r.feat.at[:, cut], r.local_sem.at[3 + 2 * i]))
        parts_w[i].start()
        parts_f[i].start()
    copy_q = pltpu.make_async_copy(r.interests, r.q, r.local_sem.at[0])
    copy_q.start()
    barrier = pltpu.get_barrier_semaphore()

    def greet(device):
        pl.semaphore_signal(barrier, inc=1, device_id=device, device_id_type=MESH)

    for d in range(1, ny):
        greet(y_peer(d))
    greet(sibling)
    greet(x_peer(1))
    greet(x_peer(-1))

    def greet_z(d, carry):
        greet(z_peer(d))
        return carry

    lax.fori_loop(1, NZ, greet_z, 0)

    own_counts = jnp.where(lax.broadcasted_iota(jnp.int32, (8, TILE), 0) == 0, r.valid[0], r.valid[1])
    r.cnt[y] = own_counts
    embedded = jnp.zeros((items, r.w.shape[1]), F32)
    for i in range(DEPTHS):
        parts_w[i].wait()
        parts_f[i].wait()
        cut = slice(i * depth, (i + 1) * depth)
        embedded = embedded + dot(r.feat[:, cut], r.w[cut, :], (1, 0))
    r.cat[0:2] = embedded.astype(BF16).reshape(2, TILE, r.w.shape[1])
    pl.semaphore_wait(barrier, (ny - 1) + 1 + 2 + (NZ - 1))

    gather = {}

    piece = 2 * TILE // PIECES
    per_tile = PIECES // 2

    def pass_on(up, step, part):
        here, there = (step - 1, step) if up else ((ny - step + 1) % ny, ny - step)
        way, slot = (0 if up else 1), PIECES * (step - 1) + part
        rows = pl.ds(part % per_tile * piece, piece)
        tile = part // per_tile
        gather[up, step, part] = send(
            r.cat.at[2 * here + tile, rows],
            r.cat.at[2 * there + tile, rows],
            r.gather_send.at[way, slot],
            r.gather_recv.at[way, slot],
            y_peer(1 if up else -1),
        )

    for part in range(PIECES):
        pass_on(True, 1, part)
        pass_on(False, 1, PIECES - 1 - part)
    counts = [
        send(r.cnt.at[y], r.cnt.at[y], r.cnt_send.at[d], r.cnt_recv.at[d], y_peer(d)) for d in range(1, ny)
    ]

    copy_q.wait()
    r.qs[...] = (r.q[...].astype(F32) * r.q.shape[1] ** -0.5).astype(BF16)
    owner_of_lane = lax.broadcasted_iota(jnp.int32, (users, lanes), 1) // kk
    of_user = owner_of_lane == lax.broadcasted_iota(jnp.int32, (users, lanes), 0)
    diagonal = lax.broadcasted_iota(jnp.int32, (users, users), 0) == lax.broadcasted_iota(
        jnp.int32, (users, users), 1
    )

    def to_lanes(column):
        return jnp.sum(jnp.where(of_user, column, 0.0), axis=0, keepdims=True)

    def to_row(values):
        spread = jnp.broadcast_to(values.astype(F32), (users, users))
        column = jnp.sum(jnp.where(diagonal, spread, 0.0), axis=1, keepdims=True)
        return to_lanes(column).astype(jnp.int32)

    n_neg = r.negatives.shape[0]
    for j in range(n_neg):
        r.neg_rows[j : j + 1, :] = to_row(r.negatives[j : j + 1, :])
    pos_row = to_row(r.positives[...])

    def origin(block):
        return lax.rem(y - block + ny, ny)

    def positive_slot(block, tile):
        first = (origin(block) * 2 + tile) * TILE
        return pos_row - first

    def fold(values, op):
        parts = values.reshape(ROWS // 8, 8, lanes)
        return op(parts, axis=0)

    def row_ids(i):
        return lax.broadcasted_iota(jnp.int32, (ROWS, lanes), 0) + i * ROWS

    counted = {0}

    def score_tile(block, tile):
        if block not in counted:
            counts[block - 1].wait_recv()
            counted.add(block)
        u = origin(block)
        index = 2 * block + tile
        first = tile * TILE
        r.expo[block, first : first + TILE, :] = dot(r.cat[index], r.qs[...], (1, 1))
        number = u * 2 + tile
        hit = jnp.zeros((1, lanes), F32)
        for j in range(n_neg):
            hit = hit + jnp.where(r.neg_rows[j : j + 1, :] == number, 1.0, 0.0)
        live = r.cnt[u][tile : tile + 1, :]
        live = jnp.concatenate([live] * (lanes // TILE), axis=1)
        live = jnp.where(hit > 0, live, 0)
        slot = positive_slot(block, tile)

        def mask(i, carry):
            peak, picked = carry
            rows = pl.ds(first + i * ROWS, ROWS)
            s = r.expo[block, rows, :]
            ids = row_ids(i)
            kept = jnp.where(ids < live, s, LOW)
            r.expo[block, rows, :] = kept
            picked = picked + fold(jnp.where(ids == slot, s, 0.0), jnp.sum)
            return jnp.maximum(peak, fold(kept, jnp.max)), picked

        peak, picked = lax.fori_loop(
            0, TILE // ROWS, mask, (jnp.full((8, lanes), LOW, F32), jnp.zeros((8, lanes), F32))
        )
        m = jnp.max(peak, axis=0, keepdims=True)

        def exponent(i, total):
            rows = pl.ds(first + i * ROWS, ROWS)
            e = hit * jnp.exp(r.expo[block, rows, :] - m)
            r.expo[block, rows, :] = e
            return total + fold(e, jnp.sum)

        total = lax.fori_loop(0, TILE // ROWS, exponent, jnp.zeros((8, lanes), F32))
        r.m_rows[index : index + 1, :] = m
        r.l_rows[index : index + 1, :] = jnp.sum(total, axis=0, keepdims=True)
        r.p_rows[index : index + 1, :] = jnp.sum(picked, axis=0, keepdims=True)

    def transpose_features(x2):
        depth = r.feat.shape[1] // NX
        turned = r.feat[:, x2 * depth : (x2 + 1) * depth].T.reshape(NZ, NC, 16, items)
        for c in range(NC):
            part = turned[:, c].reshape(NZ * 16, items)
            r.feat_t[c, x2 * NZ * 16 : (x2 + 1) * NZ * 16, :] = part

    score_tile(0, 0)
    score_tile(0, 1)
    ready = []
    turns = list(range(NX))
    for step in range(1, half + 1):
        for i in range(PIECES if step < half else per_tile):
            for up, part in ((True, i), (False, PIECES - 1 - i)):
                gather[up, step, part].wait_recv()
                if step + 1 < half or (step + 1 == half and i < per_tile):
                    pass_on(up, step + 1, part)
            if ready:
                score_tile(*ready.pop(0))
            if turns:
                transpose_features(turns.pop(0))
            if i % per_tile == per_tile - 1:
                ready += [(step, i // per_tile), ((ny - step) % ny, 1 - i // per_tile)]
    for x2 in turns:
        transpose_features(x2)
    feat_copy = send(r.feat_t.at[1 - core], r.feat_s, r.core_send.at[2], r.core_recv.at[2], sibling)
    for block, tile in ready:
        score_tile(block, tile)
    m_all = r.m_rows[...]
    pos_score = jnp.sum(r.p_rows[...], axis=0, keepdims=True)
    highest = jnp.maximum(pos_score, jnp.max(m_all, axis=0, keepdims=True))
    factor = jnp.exp(m_all - highest)
    pos_term = jnp.exp(pos_score - highest)
    denominator = pos_term + jnp.sum(factor * r.l_rows[...], axis=0, keepdims=True)
    r.m_rows[...] = factor / denominator
    pos_grad = pos_term / denominator - 1.0

    def grad_block(block):
        for tile in range(2):
            share = r.m_rows[2 * block + tile : 2 * block + tile + 1, :]
            slot = positive_slot(block, tile)

            def normalise(i, carry, tile=tile, slot=slot, share=share):
                first = tile * TILE + i * ROWS
                e = r.expo[block, pl.ds(first, ROWS), :]
                g = e * share + jnp.where(row_ids(i) == slot, pos_grad, 0.0)
                r.prob[pl.ds(block * 2 * TILE + first, ROWS), :] = g.astype(BF16)
                return carry

            lax.fori_loop(0, TILE // ROWS, normalise, 0)
        part = dot(r.prob[block * 2 * TILE : (block + 1) * 2 * TILE, :], r.q[...], (1, 0)).astype(BF16)
        r.item_part[block, 0] = part[:, :TILE]
        r.item_part[block, 1] = part[:, TILE:]

    arms = {}

    def own_block(up, k):
        return (ny - half + k) if up else (half - k)

    part_rows = items // 2

    def landing(up, k, h, v):
        return (r.ring_up if up else r.ring_down).at[2 * k + h, pl.ds(v * part_rows, part_rows)]

    def ring(up, k, h, v):
        way = 0 if up else 1
        slot = 4 * k + 2 * h + v
        arms[up, k, h, v] = send(
            r.item_part.at[own_block(up, k) % ny, h, pl.ds(v * part_rows, part_rows)],
            landing(up, k, h, v),
            r.ring_send.at[way, slot],
            r.ring_recv.at[way, slot],
            y_peer(1 if up else -1),
        )

    def arrived(up, k, h, v):
        arms[up, k, h, v].wait_recv()
        return landing(up, k, h, v)[...].astype(F32)

    def add_and_ring(up, k, h):
        block = own_block(up, k) % ny
        for v in range(2):
            own = r.item_part.at[block, h, pl.ds(v * part_rows, part_rows)]
            own[...] = (own[...].astype(F32) + arrived(up, k - 1, h, v)).astype(BF16)
            ring(up, k, h, v)

    def ring_own(up, k, h):
        for v in range(2):
            ring(up, k, h, v)

    grad_block(half)
    ring_own(True, 0, 0)
    ring_own(False, 0, 1)
    grad_block(own_block(True, 1))
    ring_own(True, 1, 1)
    grad_block(own_block(False, 1))
    ring_own(False, 1, 0)
    grad_block(own_block(True, 2))
    add_and_ring(True, 1, 0)
    add_and_ring(False, 1, 1)
    grad_block(own_block(False, 2))

    def query_part(blocks, first):
        rows = 2 * TILE
        total = None
        for block in blocks:
            c = r.cat[2 * block : 2 * block + 2].reshape(rows, r.q.shape[1])
            part = dot(r.prob[block * rows : (block + 1) * rows, :], c, (0, 0))
            total = part if total is None else total + part
        r.query_grad[...] = total if first else r.query_grad[...] + total

    for k in range(2, half):
        add_and_ring(True, k, 1)
        add_and_ring(False, k, 0)
        if k + 1 < half:
            grad_block(own_block(True, k + 1))
        else:
            query_part(range(half - 2, half + 1), True)
        add_and_ring(True, k, 0)
        add_and_ring(False, k, 1)
        if k + 1 < half:
            grad_block(own_block(False, k + 1))
    grad_block(0)
    copy_g = pltpu.make_async_copy(r.query_grad, r.grad_interests, r.local_sem.at[1])
    others = [b for b in range(ny) if not half - 2 <= b <= half]
    query_part(others[:2], False)

    def finish_queries():
        query_part(others[2:], False)
        copy_g.start()
        loss_row = highest + jnp.log(denominator) - pos_score
        loss_column = jnp.sum(jnp.where(of_user, loss_row, 0.0), axis=1, keepdims=True)
        r.user_loss[...] = jnp.sum(jnp.where(diagonal, loss_column, 0.0), axis=0, keepdims=True)

    block_rows = NZ * 16
    mid = block_rows // 2
    core_copy, x_copy = {}, {}

    def weight_part(h):
        parts = []
        for v in range(2):
            own = r.item_part[0, h, v * part_rows : (v + 1) * part_rows, :].astype(F32)
            parts.append(own + arrived(True, half - 1, h, v) + arrived(False, half - 1, h, v))
        item_grad = jnp.concatenate(parts, axis=0).astype(BF16)
        r.item_grad[h] = item_grad
        core_copy[h] = send(r.item_grad.at[h], r.item_sib.at[h], r.core_send.at[h], r.core_recv.at[h], sibling)

    def x_send(h, kind, src, dst, up):
        x_copy[h, kind] = send(src, dst, r.x_send.at[h, kind], r.x_recv.at[h, kind], x_peer(1 if up else -1))

    def x_first(h):
        r.w_own[h] = dot(r.feat_t[core], r.item_grad[h], (1, 0))
        if h == 0:
            feat_copy.wait_recv()
        core_copy[h].wait_recv()
        r.w_own[h] = r.w_own[h] + dot(r.feat_s[...], r.item_sib[h], (1, 0))

        def block_of(owner):
            rows = pl.ds(pl.multiple_of(lax.rem(owner + NX, NX) * block_rows, block_rows), block_rows)
            return r.w_own[h, rows, :]

        r.x_two[h] = block_of(x + 2).astype(BF16)
        x_send(h, 0, r.x_two.at[h, pl.ds(0, mid)], r.xr_two_up.at[h], True)
        x_send(h, 1, r.x_two.at[h, pl.ds(mid, mid)], r.xr_two_down.at[h], False)
        r.x_up[h] = block_of(x + 1).astype(BF16)
        x_send(h, 2, r.x_up.at[h, pl.ds(mid, mid)], r.xr_up.at[h, pl.ds(mid, mid)], True)
        r.x_down[h] = block_of(x - 1).astype(BF16)
        x_send(h, 3, r.x_down.at[h, pl.ds(0, mid)], r.xr_down.at[h, pl.ds(0, mid)], False)
        r.x_own[h] = block_of(x)

    def x_second(h):
        x_copy[h, 0].wait_recv()
        r.x_up[h, pl.ds(0, mid)] = (r.x_up[h, pl.ds(0, mid)].astype(F32) + r.xr_two_up[h].astype(F32)).astype(BF16)
        x_send(h, 4, r.x_up.at[h, pl.ds(0, mid)], r.xr_up.at[h, pl.ds(0, mid)], True)
        x_copy[h, 1].wait_recv()
        r.x_down[h, pl.ds(mid, mid)] = (
            r.x_down[h, pl.ds(mid, mid)].astype(F32) + r.xr_two_down[h].astype(F32)
        ).astype(BF16)
        x_send(h, 5, r.x_down.at[h, pl.ds(mid, mid)], r.xr_down.at[h, pl.ds(mid, mid)], False)

    per_y = NZ // ny
    far_first = sorted(range(1, ny), key=lambda d: -min(d, ny - d))

    def y_stage(h):
        for kind in (2, 3, 4, 5):
            x_copy[h, kind].wait_recv()
        total = (r.x_own[h] + r.xr_up[h].astype(F32) + r.xr_down[h].astype(F32)).reshape(ny, per_y, 16, TILE)
        r.y_own[h] = total
        r.y_send[h] = total.astype(BF16)
        y_copy[h] = {
            d: send(
                r.y_send.at[h, lax.rem(y + d, ny)], r.y_recv.at[h, d], r.y_ssem.at[h, d], r.y_rsem.at[h, d], y_peer(d)
            )
            for d in far_first
        }

    def z_copy(h, i, sender):
        owner = y * per_y + i
        return pltpu.make_async_remote_copy(
            src_ref=r.z_send.at[h, i],
            dst_ref=r.z_recv.at[h, sender],
            send_sem=r.z_ssem.at[h, i],
            recv_sem=r.z_rsem.at[h, sender],
            device_id=at(y, x, owner, core),
            device_id_type=MESH,
        )

    def z_stage(h):
        total = r.y_own[h, y]
        for d in range(1, ny):
            y_copy[h][d].wait_recv()
            total = total + r.y_recv[h, d].astype(F32)
        r.z_own[h] = total
        r.z_send[h] = total.astype(BF16)
        for i in range(per_y):

            @pl.when(z != y * per_y + i)
            def _(i=i):
                z_copy(h, i, z).start()

    owns = z // per_y == y

    def g_copy(h, d):
        return pltpu.make_async_remote_copy(
            src_ref=r.g_buf.at[h],
            dst_ref=r.g_buf.at[h],
            send_sem=r.g_ssem.at[h, d],
            recv_sem=r.g_rsem.at[h],
            device_id=y_peer(d),
            device_id_type=MESH,
        )

    def g_stage(h):
        @pl.when(owns)
        def _():
            def add(d, total):
                sender = lax.rem(z + d, NZ)
                z_copy(h, 0, sender).wait_recv()
                return total + r.z_recv[h, sender].astype(F32)

            r.g_buf[h] = lax.fori_loop(1, NZ, add, r.z_own[h, lax.rem(z, per_y)])
            for d in far_first:
                g_copy(h, d).start()

    def finish(h):
        @pl.when(jnp.logical_not(owns))
        def _():
            g_copy(h, 1).wait_recv()

        r.grad_w[:, h * TILE : (h + 1) * TILE] = r.g_buf[h]

    y_copy = {}
    for stage in (weight_part, x_first, x_second, y_stage, z_stage, g_stage, finish):
        for h in range(2):
            stage(h)
        if stage is x_first:
            finish_queries()

    for copy in pending:
        copy.wait_send()

    for h in range(2):
        for i in range(per_y):

            @pl.when(z != y * per_y + i)
            def _(h=h, i=i):
                z_copy(h, i, z).wait_send()

    @pl.when(owns)
    def _():
        for h in range(2):
            for d in range(1, ny):
                g_copy(h, d).wait_send()

    copy_g.wait()


def local(ny, features, w_out, interests, neg_tiles, positives, tile_valid):
    items, depth = features.shape
    width = w_out.shape[1]
    users, kk, _ = interests.shape
    lanes = users * kk
    rows = depth // (NX * NZ * NC)
    half_rows = NX * NZ * rows
    block = NZ * rows
    vmem, dma = pltpu.VMEM, pltpu.SemaphoreType.DMA
    scratch = [
        vmem((items, depth), BF16),
        vmem((NC, half_rows, items), BF16),
        vmem((depth, width), BF16),
        vmem((lanes, width), BF16),
        vmem((lanes, width), BF16),
        vmem((2 * ny, TILE, width), BF16),
        vmem((ny, 8, TILE), jnp.int32),
        vmem((8, lanes), jnp.int32),
        vmem((ny, items, lanes), F32),
        vmem((ny * items, lanes), BF16),
        vmem((2 * ny, lanes), F32),
        vmem((2 * ny, lanes), F32),
        vmem((2 * ny, lanes), F32),
        vmem((lanes, width), F32),
        vmem((ny, 2, items, TILE), BF16),
        vmem((2, items, TILE), BF16),
        vmem((ny, items, TILE), BF16),
        vmem((ny, items, TILE), BF16),
        vmem((half_rows, items), BF16),
        vmem((2, items, TILE), BF16),
        vmem((2, half_rows, TILE), F32),
        vmem((2, block, TILE), BF16),
        vmem((2, block, TILE), BF16),
        vmem((2, block, TILE), BF16),
        vmem((2, block, TILE), F32),
        vmem((2, block // 2, TILE), BF16),
        vmem((2, block // 2, TILE), BF16),
        vmem((2, block, TILE), BF16),
        vmem((2, block, TILE), BF16),
        vmem((2, ny, NZ // ny, rows, TILE), BF16),
        vmem((2, ny, NZ // ny, rows, TILE), F32),
        vmem((2, ny, NZ // ny, rows, TILE), BF16),
        vmem((2, NZ // ny, rows, TILE), BF16),
        vmem((2, NZ // ny, rows, TILE), F32),
        vmem((2, NZ, rows, TILE), BF16),
        vmem((2, rows, TILE), F32),
        dma((2 + 2 * DEPTHS,)),
        dma((ny,)),
        dma((ny,)),
        dma((2, PIECES * ny // 2)),
        dma((2, PIECES * ny // 2)),
        dma((2, 2 * ny)),
        dma((2, 2 * ny)),
        dma((3,)),
        dma((3,)),
        dma((2, 6)),
        dma((2, 6)),
        dma((2, ny)),
        dma((2, ny)),
        dma((2, NZ // ny)),
        dma((2, NZ)),
        dma((2, ny)),
        dma((2,)),
    ]
    hbm = pl.BlockSpec(memory_space=pl.ANY)
    in_vmem = pl.BlockSpec(memory_space=pltpu.VMEM)
    grad_w, query_grads, loss = pl.pallas_call(
        functools.partial(kernel, ny),
        out_shape=(
            jax.ShapeDtypeStruct((rows, width), F32),
            jax.ShapeDtypeStruct((lanes, width), F32),
            jax.ShapeDtypeStruct((1, users), F32),
        ),
        in_specs=[hbm, hbm, hbm, in_vmem, in_vmem, pl.BlockSpec(memory_space=pltpu.SMEM)],
        out_specs=(in_vmem, hbm, in_vmem),
        scratch_shapes=scratch,
        compiler_params=pltpu.CompilerParams(
            collective_id=0, has_side_effects=True, vmem_limit_bytes=53 * 1024 * 1024
        ),
    )(features, w_out, interests.reshape(lanes, width), neg_tiles.T, positives.reshape(1, users), tile_valid)
    return grad_w, query_grads.reshape(users, kk, width), loss.reshape(users)


def solution(mesh):
    in_specs = (
        P(("user", "item"), None),
        P(),
        P(("user", "item"), None, None),
        P(("user", "item"), None),
        P(("user", "item")),
        P(("user", "item")),
    )
    out_specs = (P("item", None), P(("user", "item"), None, None), P(("user", "item")))
    body = functools.partial(local, mesh.shape["user"])
    return jax.shard_map(body, mesh=mesh, in_specs=in_specs, out_specs=out_specs, check_vma=False)
```
